32 devices in a mesh: pipe: 2 (over x), expert: 16 (over z, y, core).
Axes of the slice: x: 2, y: 2, z: 4, core: 2. Of those that a mesh axis runs over, the one named last changes fastest.
Arguments:
- grad_out: bfloat16 [2, 2048, 2048], P('pipe', 'expert'), may hold values from -6 to 6
- expert_ids: int32 [2, 2048, 8], P('pipe', 'expert'), may hold values from 0 to 31, as said below
- slot_ids: int32 [2, 2048, 8], P('pipe', 'expert'), may hold values from 0 to 32, as said below
- gate_weights: float32 [2, 2048, 8], P('pipe', 'expert'), may hold values from 0.02 to 0.6
- saved_pre: bfloat16 [2, 32, 512, 1536], P('pipe', 'expert'), may hold values from -6 to 6
- down_weight: bfloat16 [2, 32, 768, 2048], P('pipe', 'expert'), may hold values from -0.21875 to 0.21875
- router_weight: bfloat16 [2, 32, 2048], P('pipe', 'expert'), may hold values from -0.125 to 0.125
Outputs:
- pre_grad: bfloat16 [2, 32, 512, 1536], P('pipe', 'expert')
- grad_inputs: bfloat16 [2, 2048, 2048], P('pipe', 'expert')
The draws below stay inside these ranges and needn't reach their ends.
Inputs may be any that keep to these rules, and one draw needn't show every extreme that they name: `expert_ids`: each row names 8 different experts. `slot_ids`: for the pair (t, k): the number of earlier pairs (by row, then by k) among the same device's 128 rows of that section that name the same expert, capped at 32; the value 32 marks a pair that is dropped.
All inputs are finite; a program needn't handle non-finite values.
Results may differ from the reference program's by a relative error of at most 0.012.
Values may be sent and summed in bfloat16 or wider, within the bound.
A program may use at most 128 MiB of HBM per device.

```python
import math
import jax
import jax.numpy as jnp
from jax import lax

D = 2048
FF = 768
TOP = 8
TOK_DEV = 128
EXPERTS = 32
TOKENS = 2048
CAP = 32
SLOTS = 512
SECTIONS = 2


def route_tables(key):
    base_key = jax.random.fold_in(key, 11)
    noise_key, level_key, hot_key = jax.random.split(base_key, 3)
    noise = jax.random.randint(noise_key, (SECTIONS, TOKENS, EXPERTS), 0, 2 ** 20)
    levels = jax.random.randint(level_key, (SECTIONS, 1, EXPERTS), 0, 3) * 2 ** 18
    hottest = jax.random.randint(hot_key, (SECTIONS, 1, 1), 0, EXPERTS)
    columns = jnp.arange(EXPERTS, dtype=jnp.int32)
    boost = jnp.where(columns[None, None, :] == hottest, 2 ** 21, 0)
    scores = (noise + levels + boost) * EXPERTS + columns[None, None, :]
    top_values, chosen = lax.top_k(scores.astype(jnp.int32), TOP)
    chosen = chosen.astype(jnp.int32)
    blocks = chosen.reshape(SECTIONS, TOKENS // TOK_DEV, TOK_DEV * TOP)
    onehot = (blocks[..., None] == columns).astype(jnp.int32)
    running = jnp.cumsum(onehot, axis=2)
    ranking = jnp.sum(onehot * running, axis=-1) - 1
    placed = jnp.minimum(ranking, CAP).reshape(SECTIONS, TOKENS, TOP)
    return (chosen, placed.astype(jnp.int32))


def draw_expert_ids(key, part):
    return route_tables(key)[0]


def draw_slot_ids(key, part):
    return route_tables(key)[1]


def level_of(rng, dims, shards, smallest, largest):
    level, own = 1.0, jax.random.fold_in(rng, 6)
    for position, shards_of in shards:
        steps = jnp.exp(jax.random.uniform(jax.random.fold_in(own, position), (shards_of,), jnp.float32, smallest / len(shards), largest / len(shards)))
        level = level * jnp.repeat(steps, dims[position] // shards_of).reshape([-1 if axis == position else 1 for axis in range(len(dims))])
    return level


def bell_draw(own_key, dims, width, bound, shards=(), held_as=jnp.bfloat16):
    drawn = width * jax.random.normal(own_key, dims, jnp.float32)
    if shards:
        drawn = drawn * level_of(own_key, dims, shards, -0.22, 0.18)
    return jnp.clip(drawn, -bound, bound).astype(held_as)


def setup_inputs(seed: int = 0) -> dict:
    keys = jax.random.split(jax.random.key(seed), 8)
    return {
        "grad_out": bell_draw(keys[0], (SECTIONS, TOKENS, D), 1.0, 6.0, ((0, 2), (1, 16))),
        "expert_ids": draw_expert_ids(jax.random.fold_in(keys[7], 71), 0),
        "slot_ids": draw_slot_ids(jax.random.fold_in(keys[7], 71), 0),
        "gate_weights": jnp.clip(jnp.exp(math.log(0.6) - 3.4011974 * jax.random.uniform(keys[3], (SECTIONS, TOKENS, TOP), jnp.float32) ** level_of(keys[3], (SECTIONS, TOKENS, TOP), ((0, 2), (1, 16)), -0.2, 0.2)), 0.02, 0.6),
        "saved_pre": bell_draw(keys[4], (SECTIONS, EXPERTS, SLOTS, 2 * FF), 1.0, 6.0, ((0, 2), (1, 16))),
        "down_weight": bell_draw(keys[5], (SECTIONS, EXPERTS, FF, D), FF ** -0.5, 0.21875, ((0, 2), (1, 16))),
        "router_weight": bell_draw(keys[6], (SECTIONS, EXPERTS, D), D ** -0.5, 0.125, ((0, 2), (1, 16))),
    }


def section_backward(operands):
    grad_out, expert_ids, slot_ids, gate_weights, saved_pre, down_weight, router_weight = operands
    kept_pairs = slot_ids < CAP
    source = (jnp.arange(TOKENS, dtype=jnp.int32) // TOK_DEV)[:, None]
    row_index = expert_ids * SLOTS + source * CAP + jnp.minimum(slot_ids, CAP - 1)
    flat_rows = jnp.where(kept_pairs, row_index, EXPERTS * SLOTS).reshape(-1).astype(jnp.int32)
    gate_low = gate_weights.astype(jnp.bfloat16)
    gate_part = saved_pre[..., :FF].astype(jnp.float32)
    up_part = saved_pre[..., FF:].astype(jnp.float32)
    sigmoid_gate = jax.nn.sigmoid(gate_part)
    silu_gate = gate_part * sigmoid_gate
    hidden = (silu_gate * up_part).astype(jnp.bfloat16)
    weights = down_weight.astype(jnp.float32)
    expert_out = jnp.einsum("esf,efd->esd", hidden.astype(jnp.float32), weights).astype(jnp.bfloat16)
    flat_out = expert_out.reshape(EXPERTS * SLOTS, D)
    pair_out = jnp.take(flat_out, flat_rows, axis=0, mode="fill", fill_value=0)
    features = grad_out.astype(jnp.float32)
    pair_scores = jnp.sum(pair_out.reshape(TOKENS, TOP, D).astype(jnp.float32) * features[:, None, :], axis=-1)
    scaled = (gate_low.astype(jnp.float32)[:, :, None] * features[:, None, :]).astype(jnp.bfloat16)
    scaled_rows = jnp.zeros((EXPERTS * SLOTS, D), jnp.bfloat16).at[flat_rows].set(scaled.reshape(TOKENS * TOP, D), mode="drop")
    scaled_rows = scaled_rows.reshape(EXPERTS, SLOTS, D)
    row_grad = jnp.einsum("esd,efd->esf", scaled_rows.astype(jnp.float32), weights)
    gate_grad = row_grad * up_part * sigmoid_gate * (1.0 + gate_part * (1.0 - sigmoid_gate))
    up_grad = row_grad * silu_gate
    pre_grad = jnp.concatenate([gate_grad, up_grad], axis=-1).astype(jnp.bfloat16)
    weighted_sum = jnp.sum(gate_weights * pair_scores, axis=-1, keepdims=True)
    select_grad = gate_weights * (pair_scores - weighted_sum)
    columns = jnp.arange(EXPERTS, dtype=jnp.int32)
    matches = expert_ids[:, :, None] == columns[None, None, :]
    logit_grad = jnp.sum(jnp.where(matches, select_grad[:, :, None], jnp.float32(0.0)), axis=1).astype(jnp.bfloat16)
    router_part = jnp.dot(logit_grad, router_weight, preferred_element_type=jnp.float32)
    section_grad = (features + router_part).astype(jnp.bfloat16)
    return pre_grad, section_grad


def reference(grad_out, expert_ids, slot_ids, gate_weights, saved_pre, down_weight, router_weight):
    pre_grad, section_grad = lax.map(section_backward, (grad_out, expert_ids, slot_ids, gate_weights, saved_pre, down_weight, router_weight))
    grad_inputs = jnp.roll(section_grad, -1, axis=0)
    return pre_grad, grad_inputs
```

```python
import functools

import jax
import jax.numpy as jnp
from jax import lax
from jax.experimental import pallas as pl
from jax.experimental.pallas import tpu as pltpu
from jax.sharding import PartitionSpec as P

MESH = pl.DeviceIdType.MESH
LAYERS = 4
CHUNKS = 4
REPEAT = 8


def kernel(
    groups, pipes, cap,
    ids_ref, slots_ref, gates_ref, x_ref, router_ref, pre_ref, w_ref,
    out_ref, grad_ref,
    xbuf, wbuf, pbuf, fa, fs, sbuf, obuf, gbuf, nbuf, nids, ngates, rbuf, own_tab, tab, ts_out, ts_in, full_gate,
    local_sem, out_sem, x_send, x_recv, tab_send, tab_recv, near_send, near_recv, router_send, router_recv, ts_send, ts_recv,
):
    experts, width, features = w_ref.shape
    tok = x_ref.shape[0]
    top = ids_ref.shape[0]
    wide = groups // (2 * LAYERS)
    near_blocks = 2 * wide
    layer_rows = near_blocks * cap
    chunk = tok // CHUNKS
    tile = experts * REPEAT
    part = features // REPEAT

    pipe = lax.axis_index("pipe")
    me = lax.axis_index("expert")
    core = me % 2
    across = (me // 2) % wide
    layer = me // near_blocks
    before = (pipe + pipes - 1) % pipes
    after = (pipe + 1) % pipes
    sibling = layer * near_blocks + across * 2 + (1 - core)

    def other_layer(step):
        low = (layer % 2 + step % 2) % 2
        high = (layer // 2 + step // 2) % 2
        return high * 2 + low

    def block_of(at_layer, at_across, at_core):
        return at_layer * near_blocks + at_across * 2 + at_core

    load_x = pltpu.make_async_copy(x_ref, xbuf.at[me], local_sem.at[0])
    load_p = pltpu.make_async_copy(pre_ref, pbuf, local_sem.at[1])
    load_w = pltpu.make_async_copy(w_ref, wbuf, local_sem.at[2])
    load_x.start()
    load_p.start()
    load_w.start()

    barrier = pltpu.get_barrier_semaphore()

    def greet_peer(i, carry):
        pl.semaphore_signal(barrier, inc=1, device_id=(pipe, (me + i) % groups), device_id_type=MESH)
        return carry

    lax.fori_loop(1, groups, greet_peer, 0)

    def greet_before(i, carry):
        pl.semaphore_signal(barrier, inc=1, device_id=(before, (me + i) % groups), device_id_type=MESH)
        return carry

    lax.fori_loop(0, groups, greet_before, 0)
    greetings = 2 * groups - 1
    if pipes > 2:
        def greet_after(i, carry):
            pl.semaphore_signal(barrier, inc=1, device_id=(after, (me + i) % groups), device_id_type=MESH)
            return carry

        lax.fori_loop(0, groups, greet_after, 0)
        greetings += groups

    rows = lax.broadcasted_iota(jnp.int32, (groups * tile, tok), 0)
    row_expert = rows // REPEAT
    gate_acc = jnp.zeros((groups * tile, tok), jnp.float32)
    slot_acc = jnp.full((groups * tile, tok), -1.0, jnp.float32)
    for k in range(top):
        slot_k = slots_ref[k : k + 1, :]
        hit = (ids_ref[k : k + 1, :] == row_expert) & (slot_k < cap)
        low_k = gates_ref[k : k + 1, :].astype(jnp.bfloat16).astype(jnp.float32)
        gate_acc = jnp.where(hit, low_k, gate_acc)
        slot_acc = jnp.where(hit, slot_k.astype(jnp.float32), slot_acc)
    table = jnp.where(rows % REPEAT < REPEAT // 2, gate_acc, slot_acc)
    own_tab[...] = table.reshape(groups, tile, tok)

    pl.semaphore_wait(barrier, greetings)

    def x_copy(source, block, start, target):
        return pltpu.make_async_remote_copy(
            src_ref=source,
            dst_ref=xbuf.at[block, pl.ds(start, chunk)],
            send_sem=x_send.at[0],
            recv_sem=x_recv.at[block, start // chunk],
            device_id=(pipe, target),
            device_id_type=MESH,
        )

    for i in range(CHUNKS):
        source = x_ref.at[pl.ds(i * chunk, chunk)]
        for step in range(1, LAYERS):
            x_copy(source, me, i * chunk, block_of(other_layer(step), across, core)).start()
        for q in range(1, wide):
            x_copy(source, me, i * chunk, block_of(layer, (across + q) % wide, core)).start()
        x_copy(source, me, i * chunk, sibling).start()

    def send_table(i, carry):
        to = (me + i) % groups
        pltpu.make_async_remote_copy(
            src_ref=own_tab.at[to], dst_ref=tab.at[me], send_sem=tab_send.at[0], recv_sem=tab_recv.at[0],
            device_id=(pipe, to), device_id_type=MESH,
        ).start()
        return carry

    lax.fori_loop(1, groups, send_table, 0)
    tab[me] = own_tab[me]

    near = [
        pltpu.make_async_remote_copy(
            src_ref=source, dst_ref=target, send_sem=near_send.at[n], recv_sem=near_recv.at[n],
            device_id=(before, me), device_id_type=MESH,
        )
        for n, (source, target) in enumerate(((ids_ref, nids), (gates_ref, ngates), (x_ref, nbuf)))
    ]
    for copy in near:
        copy.start()

    def send_router(i, carry):
        to = (me + i) % groups
        pltpu.make_async_remote_copy(
            src_ref=router_ref, dst_ref=rbuf.at[me], send_sem=router_send.at[0], recv_sem=router_recv.at[0],
            device_id=(before, to), device_id_type=MESH,
        ).start()
        return carry

    lax.fori_loop(0, groups, send_router, 0)

    load_p.wait()
    step_rows = 64

    def factors(n, carry):
        at = pl.ds(pl.multiple_of(n * step_rows, step_rows), step_rows)
        for j in range(experts):
            a = pbuf[j, at, :width].astype(jnp.float32)
            b = pbuf[j, at, width:].astype(jnp.float32)
            s = jax.nn.sigmoid(a)
            fs[j, at, :] = a * s
            fa[j, at, :] = b * s * (1.0 + a * (1.0 - s))
        return carry

    lax.fori_loop(0, pbuf.shape[1] // step_rows, factors, 0)
    load_w.wait()
    load_x.wait()
    pltpu.make_async_copy(own_tab.at[pl.ds(0, groups - 1)], tab.at[pl.ds(0, groups - 1)], tab_recv.at[0]).wait()

    def arrived(block, start):
        view = xbuf.at[block, pl.ds(start, chunk)]
        pltpu.make_async_copy(view, view, x_recv.at[block, start // chunk]).wait()

    slot_rows = lax.broadcasted_iota(jnp.int32, (cap, tok), 0).astype(jnp.float32)

    def round_of(step, carry):
        here = other_layer(step)
        after_layer = other_layer(step + 1)

        def service(i, inner):
            start = pl.multiple_of(i * chunk, chunk)

            @pl.when(step < LAYERS - 1)
            def _():
                block = block_of(after_layer, across, core)
                arrived(block, start)
                view = xbuf.at[block, pl.ds(start, chunk)]
                for q in range(1, wide):
                    x_copy(view, block, start, block_of(layer, (across + q) % wide, core)).start()
                x_copy(view, block, start, sibling).start()

            for q in range(1, wide):
                block = block_of(here, (across + q) % wide, core)
                arrived(block, start)
                x_copy(xbuf.at[block, pl.ds(start, chunk)], block, start, sibling).start()
            return inner

        lax.fori_loop(0, CHUNKS, service, 0)

        def settle(i, inner):
            start = pl.multiple_of(i * chunk, chunk)
            for q in range(wide):
                arrived(block_of(here, q, 1 - core), start)
            return inner

        lax.fori_loop(0, CHUNKS, settle, 0)

        for n in range(near_blocks):
            block = here * near_blocks + n
            picks = []
            for j in range(experts):
                gate_row = tab[block, j * REPEAT : j * REPEAT + 1, :]
                slot_row = tab[block, j * REPEAT + REPEAT // 2 : j * REPEAT + REPEAT // 2 + 1, :]
                picks.append(jnp.where(slot_row == slot_rows, gate_row, 0.0).astype(jnp.bfloat16))
            picked = jnp.dot(
                jnp.concatenate(picks, axis=0), xbuf[block], preferred_element_type=jnp.float32
            ).astype(jnp.bfloat16)
            for j in range(experts):
                sbuf[j, n * cap : (n + 1) * cap, :] = picked[j * cap : (j + 1) * cap]

        at = pl.ds(pl.multiple_of(here * layer_rows, layer_rows), layer_rows)
        for j in range(experts):
            row_grad = lax.dot_general(
                sbuf[j], wbuf[j], (((1,), (1,)), ((), ())), preferred_element_type=jnp.float32
            )
            silu = fs[j, at, :]
            hidden = (silu * pbuf[j, at, width:].astype(jnp.float32)).astype(jnp.bfloat16).astype(jnp.float32)
            obuf[j, at, :width] = (row_grad * fa[j, at, :]).astype(jnp.bfloat16)
            obuf[j, at, width:] = (row_grad * silu).astype(jnp.bfloat16)
            score = jnp.sum(hidden * row_grad, axis=1, keepdims=True)
            for n in range(near_blocks):
                block = here * near_blocks + n
                slot_row = tab[block, j * REPEAT + REPEAT // 2 : j * REPEAT + REPEAT // 2 + 1, :]
                values = jnp.sum(
                    jnp.where(slot_row == slot_rows, score[n * cap : (n + 1) * cap], 0.0), axis=0, keepdims=True
                )
                ts_out[block, j * REPEAT : (j + 1) * REPEAT, :] = jnp.broadcast_to(values, (REPEAT, tok))
        for n in range(near_blocks):
            block = here * near_blocks + n
            pltpu.make_async_remote_copy(
                src_ref=ts_out.at[block], dst_ref=ts_in.at[me], send_sem=ts_send.at[0], recv_sem=ts_recv.at[0],
                device_id=(before, block), device_id_type=MESH,
            ).start()
        pltpu.make_async_copy(obuf.at[:, at, :], out_ref.at[:, at, :], out_sem.at[here]).start()
        return carry

    lax.fori_loop(0, LAYERS, round_of, 0)

    for copy in near:
        copy.wait_recv()
    gate = jnp.zeros((groups * tile, tok), jnp.float32)
    for k in range(top):
        gate = jnp.where(nids[k : k + 1, :] == row_expert, ngates[k : k + 1, :], gate)
    full_gate[...] = gate
    pltpu.make_async_copy(rbuf, rbuf, router_recv.at[0]).wait()
    pltpu.make_async_copy(ts_in, ts_in, ts_recv.at[0]).wait()
    gate = full_gate[...]
    gate_low = gate.astype(jnp.bfloat16).astype(jnp.float32)
    scaled_score = ts_in[...].reshape(groups * tile, tok)
    score = jnp.where(gate_low > 0.0, scaled_score / jnp.where(gate_low > 0.0, gate_low, 1.0), 0.0)
    total = jnp.sum(jnp.where(rows % REPEAT == 0, gate * score, 0.0), axis=0, keepdims=True)
    logit = jnp.transpose(gate * (score - total))
    lanes = lax.broadcasted_iota(jnp.int32, (tok, groups * tile), 1) % REPEAT
    router = rbuf[...].reshape(groups * tile, part)
    for d in range(REPEAT):
        left = jnp.where(lanes == d, logit, 0.0).astype(jnp.bfloat16)
        change = jnp.dot(left, router, preferred_element_type=jnp.float32)
        at = slice(d * part, (d + 1) * part)
        gbuf[:, at] = (nbuf[:, at].astype(jnp.float32) + change).astype(jnp.bfloat16)
    store = pltpu.make_async_copy(gbuf, grad_ref, local_sem.at[3])
    store.start()

    sent = xbuf.at[pl.ds(0, groups - 1)]
    pltpu.make_async_copy(sent, sent, x_send.at[0]).wait()
    pltpu.make_async_copy(own_tab.at[pl.ds(0, groups - 1)], tab.at[pl.ds(0, groups - 1)], tab_send.at[0]).wait()
    for copy in near:
        copy.wait_send()
    pltpu.make_async_copy(rbuf, rbuf, router_send.at[0]).wait()
    pltpu.make_async_copy(ts_in, ts_in, ts_send.at[0]).wait()
    for n in range(LAYERS):
        at = pl.ds(n * layer_rows, layer_rows)
        pltpu.make_async_copy(obuf.at[:, at, :], out_ref.at[:, at, :], out_sem.at[n]).wait()
    store.wait()


def per_device(grad_out, expert_ids, slot_ids, gate_weights, saved_pre, down_weight, router_weight):
    groups = lax.axis_size("expert")
    pipes = lax.axis_size("pipe")
    _, experts, width, features = down_weight.shape
    slots = saved_pre.shape[2]
    tok = grad_out.shape[1]
    top = expert_ids.shape[2]
    cap = slots // groups
    layer_rows = slots // LAYERS
    tile = experts * REPEAT
    part = features // REPEAT
    bf16, f32 = jnp.bfloat16, jnp.float32
    dma = pltpu.SemaphoreType.DMA
    vmem = pl.BlockSpec(memory_space=pltpu.VMEM)
    anywhere = pl.BlockSpec(memory_space=pl.ANY)
    pre_grad, grad_inputs = pl.pallas_call(
        functools.partial(kernel, groups, pipes, cap),
        out_shape=(
            jax.ShapeDtypeStruct((experts, slots, 2 * width), bf16),
            jax.ShapeDtypeStruct((tok, features), bf16),
        ),
        in_specs=[vmem, vmem, vmem, anywhere, vmem, anywhere, anywhere],
        out_specs=(anywhere, anywhere),
        scratch_shapes=[
            pltpu.VMEM((groups, tok, features), bf16),
            pltpu.VMEM((experts, width, features), bf16),
            pltpu.VMEM((experts, slots, 2 * width), bf16),
            pltpu.VMEM((experts, slots, width), f32),
            pltpu.VMEM((experts, slots, width), f32),
            pltpu.VMEM((experts, layer_rows, features), bf16),
            pltpu.VMEM((experts, slots, 2 * width), bf16),
            pltpu.VMEM((tok, features), bf16),
            pltpu.VMEM((tok, features), bf16),
            pltpu.VMEM((top, tok), jnp.int32),
            pltpu.VMEM((top, tok), f32),
            pltpu.VMEM((groups, tile, part), bf16),
            pltpu.VMEM((groups, tile, tok), f32),
            pltpu.VMEM((groups, tile, tok), f32),
            pltpu.VMEM((groups, tile, tok), f32),
            pltpu.VMEM((groups, tile, tok), f32),
            pltpu.VMEM((groups * tile, tok), f32),
            dma((4,)),
            dma((LAYERS,)),
            dma((1,)),
            dma((groups, CHUNKS)),
            dma((1,)),
            dma((1,)),
            dma((3,)),
            dma((3,)),
            dma((1,)),
            dma((1,)),
            dma((1,)),
            dma((1,)),
        ],
        compiler_params=pltpu.CompilerParams(
            collective_id=0, has_side_effects=True, vmem_limit_bytes=56 * 1024 * 1024
        ),
        cost_estimate=pl.CostEstimate(
            flops=2 * experts * slots * width * features, bytes_accessed=16 * 1024 * 1024, transcendentals=0
        ),
    )(
        expert_ids[0].T,
        slot_ids[0].T,
        gate_weights[0].T,
        grad_out[0],
        router_weight[0].reshape(tile, part),
        saved_pre[0],
        down_weight[0],
    )
    return (pre_grad[None], grad_inputs[None])


def solution(mesh):
    in_specs = (
        P("pipe", "expert", None),
        P("pipe", "expert", None),
        P("pipe", "expert", None),
        P("pipe", "expert", None),
        P("pipe", "expert", None, None),
        P("pipe", "expert", None, None),
        P("pipe", "expert", None),
    )
    out_specs = (P("pipe", "expert", None, None), P("pipe", "expert", None))
    return jax.shard_map(
        per_device, mesh=mesh, in_specs=in_specs, out_specs=out_specs, check_vma=False
    )
```

```python
import functools

import jax
import jax.numpy as jnp
from jax import lax
from jax.experimental import pallas as pl
from jax.experimental.pallas import tpu as pltpu
from jax.sharding import PartitionSpec as P

MESH = pl.DeviceIdType.MESH
LAYERS = 4
CHUNKS = 8
PARTS = 3
REPEAT = 8
UP, SIDE_UP, OWN_SIDE, SIDE, SIB = 0, 2, 4, 5, 6


def kernel(
    groups, pipes, cap,
    ids_ref, slots_ref, gates_ref, x_ref, router_ref, pre_ref, w_ref,
    out_ref, grad_ref,
    xbuf, wbuf, pbuf, fa, fs, sbuf, obuf, gbuf, nbuf, nids, ngates, rbuf, own_tab, tab, ts_out, ts_in, full_gate, scores,
    local_sem, out_sem, x_send, x_recv, sib_recv, tab_send, tab_recv, near_send, near_recv, router_send, router_recv, ts_send, ts_recv,
):
    experts, width, features = w_ref.shape
    tok = x_ref.shape[0]
    top = ids_ref.shape[0]
    wide = groups // (2 * LAYERS)
    near_blocks = 2 * wide
    layer_rows = near_blocks * cap
    chunk = tok // CHUNKS
    tile = experts * REPEAT
    part = features // REPEAT

    pipe = lax.axis_index("pipe")
    me = lax.axis_index("expert")
    core = me % 2
    across = (me // 2) % wide
    layer = me // near_blocks
    before = (pipe + pipes - 1) % pipes
    after = (pipe + 1) % pipes
    sibling = layer * near_blocks + across * 2 + (1 - core)

    def block_of(at_layer, at_across, at_core):
        return at_layer * near_blocks + at_across * 2 + at_core

    inner_layer = ((layer + 1) // 2) % 2
    flip = layer // 2

    def order(p):
        base = (1 - inner_layer) * p + inner_layer * ((p + 1) % 3 + 2 * (p // 3))
        first = (1 - (p + LAYERS - 1) // LAYERS) * layer
        other = (1 - flip) * base + flip * (LAYERS - 1 - base)
        return first + ((p + LAYERS - 1) // LAYERS) * other

    load_x = pltpu.make_async_copy(x_ref, xbuf.at[me], local_sem.at[0])
    load_p = pltpu.make_async_copy(pre_ref, pbuf, local_sem.at[1])
    load_w = pltpu.make_async_copy(w_ref, wbuf, local_sem.at[2])
    load_x.start()
    load_p.start()
    load_w.start()

    barrier = pltpu.get_barrier_semaphore()

    def greet_peer(i, carry):
        pl.semaphore_signal(barrier, inc=1, device_id=(pipe, (me + i) % groups), device_id_type=MESH)
        return carry

    lax.fori_loop(1, groups, greet_peer, 0)

    def greet_before(i, carry):
        pl.semaphore_signal(barrier, inc=1, device_id=(before, (me + i) % groups), device_id_type=MESH)
        return carry

    lax.fori_loop(0, groups, greet_before, 0)
    greetings = 2 * groups - 1
    if pipes > 2:
        def greet_after(i, carry):
            pl.semaphore_signal(barrier, inc=1, device_id=(after, (me + i) % groups), device_id_type=MESH)
            return carry

        lax.fori_loop(0, groups, greet_after, 0)
        greetings += groups

    rows = lax.broadcasted_iota(jnp.int32, (groups * tile, tok), 0)
    row_expert = rows // REPEAT
    gate_acc = jnp.zeros((groups * tile, tok), jnp.float32)
    slot_acc = jnp.full((groups * tile, tok), -1.0, jnp.float32)
    for k in range(top):
        slot_k = slots_ref[k : k + 1, :]
        hit = (ids_ref[k : k + 1, :] == row_expert) & (slot_k < cap)
        low_k = gates_ref[k : k + 1, :].astype(jnp.bfloat16).astype(jnp.float32)
        gate_acc = jnp.where(hit, low_k, gate_acc)
        slot_acc = jnp.where(hit, slot_k.astype(jnp.float32), slot_acc)
    table = jnp.where(rows % REPEAT < REPEAT // 2, gate_acc, slot_acc)
    own_tab[...] = table.reshape(groups, tile, tok)

    pl.semaphore_wait(barrier, greetings)

    def x_copy(source, block, start, target, sent, arrives):
        return pltpu.make_async_remote_copy(
            src_ref=source,
            dst_ref=xbuf.at[block, pl.ds(start, chunk)],
            send_sem=x_send.at[sent],
            recv_sem=arrives,
            device_id=(pipe, target),
            device_id_type=MESH,
        )

    def along(source, block, start, up, down, sent):
        arrives = x_recv.at[block, start // chunk]

        @pl.when(up * (LAYERS - 1 - layer) > 0)
        def _():
            x_copy(source, block, start, me + near_blocks, sent, arrives).start()

        @pl.when(down * layer > 0)
        def _():
            x_copy(source, block, start, me - near_blocks, sent + 1, arrives).start()

    def sideways(source, block, start, sent):
        arrives = x_recv.at[block, start // chunk]
        for q in range(1, wide):
            x_copy(source, block, start, block_of(layer, (across + q) % wide, core), sent, arrives).start()

    def over(source, block, start):
        x_copy(source, block, start, sibling, SIB, sib_recv.at[block]).start()

    last = (CHUNKS - 1) * chunk
    sideways(x_ref.at[pl.ds(last, chunk)], me, last, OWN_SIDE)
    for i in range(CHUNKS):
        source = x_ref.at[pl.ds(i * chunk, chunk)]
        along(source, me, i * chunk, 1, 1, UP)
        if i < CHUNKS - 1:
            sideways(source, me, i * chunk, OWN_SIDE)
        over(source, me, i * chunk)

    def send_table(i, carry):
        to = (me + i) % groups
        pltpu.make_async_remote_copy(
            src_ref=own_tab.at[to], dst_ref=tab.at[me], send_sem=tab_send.at[0], recv_sem=tab_recv.at[0],
            device_id=(pipe, to), device_id_type=MESH,
        ).start()
        return carry

    lax.fori_loop(1, groups, send_table, 0)
    tab[me] = own_tab[me]

    near = [
        pltpu.make_async_remote_copy(
            src_ref=source, dst_ref=target, send_sem=near_send.at[n], recv_sem=near_recv.at[n],
            device_id=(before, me), device_id_type=MESH,
        )
        for n, (source, target) in enumerate(((ids_ref, nids), (gates_ref, ngates), (x_ref, nbuf)))
    ]
    for copy in near:
        copy.start()

    def send_router(i, carry):
        to = (me + i) % groups
        pltpu.make_async_remote_copy(
            src_ref=router_ref, dst_ref=rbuf.at[me], send_sem=router_send.at[0], recv_sem=router_recv.at[0],
            device_id=(before, to), device_id_type=MESH,
        ).start()
        return carry

    lax.fori_loop(0, groups, send_router, 0)

    load_p.wait()
    step_rows = 64

    def factors(n, carry):
        at = pl.ds(pl.multiple_of(n * step_rows, step_rows), step_rows)
        for j in range(experts):
            a = pbuf[j, at, :width].astype(jnp.float32)
            b = pbuf[j, at, width:].astype(jnp.float32)
            s = jax.nn.sigmoid(a)
            fs[j, at, :] = a * s
            fa[j, at, :] = b * s * (1.0 + a * (1.0 - s))
        return carry

    lax.fori_loop(0, pbuf.shape[1] // step_rows, factors, 0)
    load_w.wait()
    load_x.wait()
    pltpu.make_async_copy(own_tab.at[pl.ds(0, groups - 1)], tab.at[pl.ds(0, groups - 1)], tab_recv.at[0]).wait()

    def arrived(block, start):
        view = xbuf.at[block, pl.ds(start, chunk)]
        pltpu.make_async_copy(view, view, x_recv.at[block, start // chunk]).wait()

    slot_rows = lax.broadcasted_iota(jnp.int32, (cap, tok), 0).astype(jnp.float32)

    pick_blocks = near_blocks // 4
    part_width = width // PARTS

    def round_of(p, carry):
        here = order(p % LAYERS)
        coming = order((p + 1) % LAYERS)
        ready = order((p + LAYERS - 1) % LAYERS)
        at = pl.ds(pl.multiple_of(ready * layer_rows, layer_rows), layer_rows)
        up = (LAYERS - 1 + layer - coming) // LAYERS
        down = (LAYERS - 1 + coming - layer) // LAYERS

        @pl.when(p > 0)
        def _():
            for q in range(wide):
                view = xbuf.at[block_of(ready, q, 1 - core)]
                pltpu.make_async_copy(view, view, sib_recv.at[block_of(ready, q, 1 - core)]).wait()

        def step(i, inner):
            start = pl.multiple_of(i * chunk, chunk)

            @pl.when(p < LAYERS - 1)
            def _():
                block = block_of(coming, across, core)
                arrived(block, start)
                view = xbuf.at[block, pl.ds(start, chunk)]
                along(view, block, start, up, down, UP)

                @pl.when(i < CHUNKS - 1)
                def _():
                    sideways(view, block, start, SIDE)

                over(view, block, start)

                @pl.when(i == CHUNKS - 1)
                def _():
                    for q in range(1, wide):
                        block = block_of(coming, (across + q) % wide, core)
                        arrived(block, last)
                        view = xbuf.at[block, pl.ds(last, chunk)]
                        along(view, block, last, up, down, SIDE_UP)
                        over(view, block, last)

            @pl.when((p < LAYERS) & (i < CHUNKS - 1))
            def _():
                for q in range(1, wide):
                    block = block_of(here, (across + q) % wide, core)
                    arrived(block, start)
                    over(xbuf.at[block, pl.ds(start, chunk)], block, start)

            @pl.when((p == 0) & (i == 0))
            def _():
                for q in range(1, wide):
                    block = block_of(layer, (across + q) % wide, core)
                    arrived(block, last)
                    view = xbuf.at[block, pl.ds(last, chunk)]
                    along(view, block, last, 1, 1, SIDE_UP)
                    over(view, block, last)

            @pl.when((p > 0) & (i < 4))
            def _():
                for n in range(pick_blocks):
                    block = ready * near_blocks + i * pick_blocks + n
                    picks = []
                    for j in range(experts):
                        gate_row = tab[block, j * REPEAT : j * REPEAT + 1, :]
                        slot_row = tab[block, j * REPEAT + REPEAT // 2 : j * REPEAT + REPEAT // 2 + 1, :]
                        picks.append(jnp.where(slot_row == slot_rows, gate_row, 0.0).astype(jnp.bfloat16))
                    picked = jnp.dot(
                        jnp.concatenate(picks, axis=0), xbuf[block], preferred_element_type=jnp.float32
                    ).astype(jnp.bfloat16)
                    to = pl.ds(pl.multiple_of((i * pick_blocks + n) * cap, cap), cap)
                    for j in range(experts):
                        sbuf[j, to, :] = picked[j * cap : (j + 1) * cap]

            for m in range(PARTS):
                @pl.when((p > 0) & (i == 4 + m))
                def _():
                    left = slice(m * part_width, (m + 1) * part_width)
                    right = slice(width + m * part_width, width + (m + 1) * part_width)
                    for j in range(experts):
                        row_grad = lax.dot_general(
                            sbuf[j], wbuf[j, left], (((1,), (1,)), ((), ())), preferred_element_type=jnp.float32
                        )
                        silu = fs[j, at, left]
                        hidden = (silu * pbuf[j, at, right].astype(jnp.float32)).astype(jnp.bfloat16)
                        obuf[j, at, left] = (row_grad * fa[j, at, left]).astype(jnp.bfloat16)
                        obuf[j, at, right] = (row_grad * silu).astype(jnp.bfloat16)
                        score = jnp.sum(hidden.astype(jnp.float32) * row_grad, axis=1, keepdims=True)
                        score = jnp.broadcast_to(score, (layer_rows, tok))
                        scores[j] = score if m == 0 else scores[j] + score

            @pl.when((p > 0) & (i == 4 + PARTS))
            def _():
                for n in range(near_blocks):
                    block = ready * near_blocks + n
                    for j in range(experts):
                        slot_row = tab[block, j * REPEAT + REPEAT // 2 : j * REPEAT + REPEAT // 2 + 1, :]
                        values = jnp.sum(
                            jnp.where(slot_row == slot_rows, scores[j, n * cap : (n + 1) * cap, :], 0.0),
                            axis=0,
                            keepdims=True,
                        )
                        ts_out[block, j * REPEAT : (j + 1) * REPEAT, :] = jnp.broadcast_to(values, (REPEAT, tok))
                    pltpu.make_async_remote_copy(
                        src_ref=ts_out.at[block], dst_ref=ts_in.at[me], send_sem=ts_send.at[0], recv_sem=ts_recv.at[0],
                        device_id=(before, block), device_id_type=MESH,
                    ).start()
                pltpu.make_async_copy(obuf.at[:, at, :], out_ref.at[:, at, :], out_sem.at[ready]).start()
            return inner

        lax.fori_loop(0, CHUNKS, step, 0)
        return carry

    lax.fori_loop(0, LAYERS + 1, round_of, 0)

    for copy in near:
        copy.wait_recv()
    gate = jnp.zeros((groups * tile, tok), jnp.float32)
    for k in range(top):
        gate = jnp.where(nids[k : k + 1, :] == row_expert, ngates[k : k + 1, :], gate)
    full_gate[...] = gate
    pltpu.make_async_copy(rbuf, rbuf, router_recv.at[0]).wait()
    pltpu.make_async_copy(ts_in, ts_in, ts_recv.at[0]).wait()
    gate = full_gate[...]
    gate_low = gate.astype(jnp.bfloat16).astype(jnp.float32)
    scaled_score = ts_in[...].reshape(groups * tile, tok)
    score = jnp.where(gate_low > 0.0, scaled_score / jnp.where(gate_low > 0.0, gate_low, 1.0), 0.0)
    total = jnp.sum(jnp.where(rows % REPEAT == 0, gate * score, 0.0), axis=0, keepdims=True)
    logit = jnp.transpose(gate * (score - total))
    lanes = lax.broadcasted_iota(jnp.int32, (tok, groups * tile), 1) % REPEAT
    router = rbuf[...].reshape(groups * tile, part)
    for d in range(REPEAT):
        left = jnp.where(lanes == d, logit, 0.0).astype(jnp.bfloat16)
        change = jnp.dot(left, router, preferred_element_type=jnp.float32)
        at = slice(d * part, (d + 1) * part)
        gbuf[:, at] = (nbuf[:, at].astype(jnp.float32) + change).astype(jnp.bfloat16)
    store = pltpu.make_async_copy(gbuf, grad_ref, local_sem.at[3])
    store.start()

    def all_sent(blocks, count, sem):
        view = xbuf.at[pl.ds(0, blocks), pl.ds(0, count)]
        pltpu.make_async_copy(view, view, x_send.at[sem]).wait()

    all_sent(groups // 2, tok, SIB)
    if wide > 1:
        all_sent(wide - 1, tok, OWN_SIDE)
        all_sent((LAYERS - 1) * (wide - 1), tok - chunk, SIDE)
    for n in range(LAYERS):
        @pl.when(layer == n)
        def _():
            if n < LAYERS - 1:
                all_sent(n + 1, tok, UP)
                if wide > 1:
                    all_sent((n + 1) * (wide - 1), chunk, SIDE_UP)
            if n > 0:
                all_sent(LAYERS - n, tok, UP + 1)
                if wide > 1:
                    all_sent((LAYERS - n) * (wide - 1), chunk, SIDE_UP + 1)
    pltpu.make_async_copy(own_tab.at[pl.ds(0, groups - 1)], tab.at[pl.ds(0, groups - 1)], tab_send.at[0]).wait()
    for copy in near:
        copy.wait_send()
    pltpu.make_async_copy(rbuf, rbuf, router_send.at[0]).wait()
    pltpu.make_async_copy(ts_in, ts_in, ts_send.at[0]).wait()
    for n in range(LAYERS):
        at = pl.ds(n * layer_rows, layer_rows)
        pltpu.make_async_copy(obuf.at[:, at, :], out_ref.at[:, at, :], out_sem.at[n]).wait()
    store.wait()


def per_device(grad_out, expert_ids, slot_ids, gate_weights, saved_pre, down_weight, router_weight):
    groups = lax.axis_size("expert")
    pipes = lax.axis_size("pipe")
    _, experts, width, features = down_weight.shape
    slots = saved_pre.shape[2]
    tok = grad_out.shape[1]
    top = expert_ids.shape[2]
    cap = slots // groups
    layer_rows = slots // LAYERS
    tile = experts * REPEAT
    part = features // REPEAT
    bf16, f32 = jnp.bfloat16, jnp.float32
    dma = pltpu.SemaphoreType.DMA
    vmem = pl.BlockSpec(memory_space=pltpu.VMEM)
    anywhere = pl.BlockSpec(memory_space=pl.ANY)
    pre_grad, grad_inputs = pl.pallas_call(
        functools.partial(kernel, groups, pipes, cap),
        out_shape=(
            jax.ShapeDtypeStruct((experts, slots, 2 * width), bf16),
            jax.ShapeDtypeStruct((tok, features), bf16),
        ),
        in_specs=[vmem, vmem, vmem, anywhere, vmem, anywhere, anywhere],
        out_specs=(anywhere, anywhere),
        scratch_shapes=[
            pltpu.VMEM((groups, tok, features), bf16),
            pltpu.VMEM((experts, width, features), bf16),
            pltpu.VMEM((experts, slots, 2 * width), bf16),
            pltpu.VMEM((experts, slots, width), f32),
            pltpu.VMEM((experts, slots, width), f32),
            pltpu.VMEM((experts, layer_rows, features), bf16),
            pltpu.VMEM((experts, slots, 2 * width), bf16),
            pltpu.VMEM((tok, features), bf16),
            pltpu.VMEM((tok, features), bf16),
            pltpu.VMEM((top, tok), jnp.int32),
            pltpu.VMEM((top, tok), f32),
            pltpu.VMEM((groups, tile, part), bf16),
            pltpu.VMEM((groups, tile, tok), f32),
            pltpu.VMEM((groups, tile, tok), f32),
            pltpu.VMEM((groups, tile, tok), f32),
            pltpu.VMEM((groups, tile, tok), f32),
            pltpu.VMEM((groups * tile, tok), f32),
            pltpu.VMEM((experts, layer_rows, tok), f32),
            dma((4,)),
            dma((LAYERS,)),
            dma((7,)),
            dma((groups, CHUNKS)),
            dma((groups,)),
            dma((1,)),
            dma((1,)),
            dma((3,)),
            dma((3,)),
            dma((1,)),
            dma((1,)),
            dma((1,)),
            dma((1,)),
        ],
        compiler_params=pltpu.CompilerParams(
            collective_id=0, has_side_effects=True, vmem_limit_bytes=56 * 1024 * 1024
        ),
        cost_estimate=pl.CostEstimate(
            flops=2 * experts * slots * width * features, bytes_accessed=16 * 1024 * 1024, transcendentals=0
        ),
    )(
        expert_ids[0].T,
        slot_ids[0].T,
        gate_weights[0].T,
        grad_out[0],
        router_weight[0].reshape(tile, part),
        saved_pre[0],
        down_weight[0],
    )
    return (pre_grad[None], grad_inputs[None])


def solution(mesh):
    in_specs = (
        P("pipe", "expert", None),
        P("pipe", "expert", None),
        P("pipe", "expert", None),
        P("pipe", "expert", None),
        P("pipe", "expert", None, None),
        P("pipe", "expert", None, None),
        P("pipe", "expert", None),
    )
    out_specs = (P("pipe", "expert", None, None), P("pipe", "expert", None))
    return jax.shard_map(
        per_device, mesh=mesh, in_specs=in_specs, out_specs=out_specs, check_vma=False
    )
```

```python
import functools

import jax
import jax.numpy as jnp
from jax import lax
from jax.experimental import pallas as pl
from jax.experimental.pallas import tpu as pltpu
from jax.sharding import PartitionSpec as P

MESH = pl.DeviceIdType.MESH
LAYERS = 4
CHUNKS = 8
PARTS = 3
REPEAT = 8
UP, SIDE_UP, OWN_SIDE, SIDE, SIB = 0, 2, 4, 5, 6


def kernel(
    groups, pipes, cap,
    ids_ref, slots_ref, gates_ref, x_ref, router_ref, pre_ref, w_ref,
    out_ref, grad_ref,
    xbuf, wbuf, pbuf, fa, fs, sbuf, obuf, gbuf, nbuf, nids, ngates, rbuf, own_tab, tab, ts_out, ts_in, full_gate, scores, router_own,
    local_sem, out_sem, x_send, x_recv, sib_recv, tab_send, tab_recv, near_send, near_recv, router_send, router_recv, ts_send, ts_recv,
):
    experts, width, features = w_ref.shape
    tok = x_ref.shape[0]
    top = ids_ref.shape[0]
    wide = groups // (2 * LAYERS)
    near_blocks = 2 * wide
    layer_rows = near_blocks * cap
    chunk = tok // CHUNKS
    tile = experts * REPEAT
    part = features // REPEAT

    pipe = lax.axis_index("pipe")
    me = lax.axis_index("expert")
    core = me % 2
    across = (me // 2) % wide
    layer = me // near_blocks
    before = (pipe + pipes - 1) % pipes
    after = (pipe + 1) % pipes
    sibling = layer * near_blocks + across * 2 + (1 - core)

    def block_of(at_layer, at_across, at_core):
        return at_layer * near_blocks + at_across * 2 + at_core

    inner_layer = ((layer + 1) // 2) % 2
    flip = layer // 2

    def order(p):
        base = (1 - inner_layer) * p + inner_layer * ((p + 1) % 3 + 2 * (p // 3))
        first = (1 - (p + LAYERS - 1) // LAYERS) * layer
        other = (1 - flip) * base + flip * (LAYERS - 1 - base)
        return first + ((p + LAYERS - 1) // LAYERS) * other

    load_x = pltpu.make_async_copy(x_ref, xbuf.at[me], local_sem.at[0])
    load_p = pltpu.make_async_copy(pre_ref, pbuf, local_sem.at[1])
    load_w = pltpu.make_async_copy(w_ref, wbuf, local_sem.at[2])
    load_x.start()
    load_p.start()
    load_w.start()

    barrier = pltpu.get_barrier_semaphore()

    def greet_peer(i, carry):
        pl.semaphore_signal(barrier, inc=1, device_id=(pipe, (me + i) % groups), device_id_type=MESH)
        return carry

    lax.fori_loop(1, groups, greet_peer, 0)

    def greet_before(i, carry):
        pl.semaphore_signal(barrier, inc=1, device_id=(before, (me + i) % groups), device_id_type=MESH)
        return carry

    lax.fori_loop(0, groups, greet_before, 0)
    greetings = 2 * groups - 1
    if pipes > 2:
        def greet_after(i, carry):
            pl.semaphore_signal(barrier, inc=1, device_id=(after, (me + i) % groups), device_id_type=MESH)
            return carry

        lax.fori_loop(0, groups, greet_after, 0)
        greetings += groups

    rows = lax.broadcasted_iota(jnp.int32, (groups * tile, tok), 0)
    row_expert = rows // REPEAT
    gate_acc = jnp.zeros((groups * tile, tok), jnp.float32)
    slot_acc = jnp.full((groups * tile, tok), -1.0, jnp.float32)
    for k in range(top):
        slot_k = slots_ref[k : k + 1, :]
        hit = (ids_ref[k : k + 1, :] == row_expert) & (slot_k < cap)
        low_k = gates_ref[k : k + 1, :].astype(jnp.bfloat16).astype(jnp.float32)
        gate_acc = jnp.where(hit, low_k, gate_acc)
        slot_acc = jnp.where(hit, slot_k.astype(jnp.float32), slot_acc)
    table = jnp.where(rows % REPEAT < REPEAT // 2, gate_acc, slot_acc)
    own_tab[...] = table.reshape(groups, tile, tok)

    router_rows = router_ref[...].astype(jnp.float32)
    router_own[...] = jnp.concatenate(
        [router_rows[j : j + 1, d * part : (d + 1) * part] for j in range(experts) for d in range(REPEAT)], axis=0
    ).astype(jnp.bfloat16)

    pl.semaphore_wait(barrier, greetings)

    def x_copy(source, block, start, target, sent, arrives):
        return pltpu.make_async_remote_copy(
            src_ref=source,
            dst_ref=xbuf.at[block, pl.ds(start, chunk)],
            send_sem=x_send.at[sent],
            recv_sem=arrives,
            device_id=(pipe, target),
            device_id_type=MESH,
        )

    def along(source, block, start, up, down, sent):
        arrives = x_recv.at[block, start // chunk]

        @pl.when(up * (LAYERS - 1 - layer) > 0)
        def _():
            x_copy(source, block, start, me + near_blocks, sent, arrives).start()

        @pl.when(down * layer > 0)
        def _():
            x_copy(source, block, start, me - near_blocks, sent + 1, arrives).start()

    def sideways(source, block, start, sent):
        arrives = x_recv.at[block, start // chunk]
        for q in range(1, wide):
            x_copy(source, block, start, block_of(layer, (across + q) % wide, core), sent, arrives).start()

    def over(source, block, start):
        x_copy(source, block, start, sibling, SIB, sib_recv.at[block]).start()

    last = (CHUNKS - 1) * chunk
    sideways(x_ref.at[pl.ds(last, chunk)], me, last, OWN_SIDE)
    for i in range(CHUNKS):
        source = x_ref.at[pl.ds(i * chunk, chunk)]
        along(source, me, i * chunk, 1, 1, UP)
        if i < CHUNKS - 1:
            sideways(source, me, i * chunk, OWN_SIDE)
        over(source, me, i * chunk)

    def send_table(i, carry):
        to = (me + i) % groups
        pltpu.make_async_remote_copy(
            src_ref=own_tab.at[to], dst_ref=tab.at[me], send_sem=tab_send.at[0], recv_sem=tab_recv.at[0],
            device_id=(pipe, to), device_id_type=MESH,
        ).start()
        return carry

    lax.fori_loop(1, groups, send_table, 0)
    tab[me] = own_tab[me]

    near = [
        pltpu.make_async_remote_copy(
            src_ref=source, dst_ref=target, send_sem=near_send.at[n], recv_sem=near_recv.at[n],
            device_id=(before, me), device_id_type=MESH,
        )
        for n, (source, target) in enumerate(((ids_ref, nids), (gates_ref, ngates), (x_ref, nbuf)))
    ]
    for copy in near:
        copy.start()

    def send_router(i, carry):
        to = (me + i) % groups
        pltpu.make_async_remote_copy(
            src_ref=router_own, dst_ref=rbuf.at[me], send_sem=router_send.at[0], recv_sem=router_recv.at[0],
            device_id=(before, to), device_id_type=MESH,
        ).start()
        return carry

    lax.fori_loop(0, groups, send_router, 0)

    load_p.wait()
    factor_rows = pbuf.shape[1] // CHUNKS

    def factors(n):
        at = pl.ds(pl.multiple_of(n * factor_rows, factor_rows), factor_rows)
        for j in range(experts):
            a = pbuf[j, at, :width].astype(jnp.float32)
            b = pbuf[j, at, width:].astype(jnp.float32)
            s = jax.nn.sigmoid(a)
            fs[j, at, :] = a * s
            fa[j, at, :] = b * s * (1.0 + a * (1.0 - s))

    def arrived(block, start):
        view = xbuf.at[block, pl.ds(start, chunk)]
        pltpu.make_async_copy(view, view, x_recv.at[block, start // chunk]).wait()

    slot_rows = lax.broadcasted_iota(jnp.int32, (cap, tok), 0).astype(jnp.float32)

    pick_blocks = near_blocks // 4
    part_width = width // PARTS

    def round_of(p, carry):
        here = order(p % LAYERS)
        coming = order((p + 1) % LAYERS)
        ready = order((p + LAYERS - 1) % LAYERS)
        at = pl.ds(pl.multiple_of(ready * layer_rows, layer_rows), layer_rows)
        up = (LAYERS - 1 + layer - coming) // LAYERS
        down = (LAYERS - 1 + coming - layer) // LAYERS

        @pl.when(p == 1)
        def _():
            load_w.wait()
            load_x.wait()
            pltpu.make_async_copy(
                own_tab.at[pl.ds(0, groups - 1)], tab.at[pl.ds(0, groups - 1)], tab_recv.at[0]
            ).wait()

        @pl.when(p > 0)
        def _():
            for q in range(wide):
                view = xbuf.at[block_of(ready, q, 1 - core)]
                pltpu.make_async_copy(view, view, sib_recv.at[block_of(ready, q, 1 - core)]).wait()

        def step(i, inner):
            start = pl.multiple_of(i * chunk, chunk)

            @pl.when(p < LAYERS - 1)
            def _():
                block = block_of(coming, across, core)
                arrived(block, start)
                view = xbuf.at[block, pl.ds(start, chunk)]
                along(view, block, start, up, down, UP)

                @pl.when(i < CHUNKS - 1)
                def _():
                    sideways(view, block, start, SIDE)

                over(view, block, start)

                @pl.when(i == CHUNKS - 1)
                def _():
                    for q in range(1, wide):
                        block = block_of(coming, (across + q) % wide, core)
                        arrived(block, last)
                        view = xbuf.at[block, pl.ds(last, chunk)]
                        along(view, block, last, up, down, SIDE_UP)
                        over(view, block, last)

            @pl.when((p < LAYERS) & (i < CHUNKS - 1))
            def _():
                for q in range(1, wide):
                    block = block_of(here, (across + q) % wide, core)
                    arrived(block, start)
                    over(xbuf.at[block, pl.ds(start, chunk)], block, start)

            @pl.when((p == 0) & (i == 0))
            def _():
                for q in range(1, wide):
                    block = block_of(layer, (across + q) % wide, core)
                    arrived(block, last)
                    view = xbuf.at[block, pl.ds(last, chunk)]
                    along(view, block, last, 1, 1, SIDE_UP)
                    over(view, block, last)

            @pl.when(p == 0)
            def _():
                factors(i)

            @pl.when((p > 0) & (i < 4))
            def _():
                for n in range(pick_blocks):
                    block = ready * near_blocks + i * pick_blocks + n
                    picks = []
                    for j in range(experts):
                        gate_row = tab[block, j * REPEAT : j * REPEAT + 1, :]
                        slot_row = tab[block, j * REPEAT + REPEAT // 2 : j * REPEAT + REPEAT // 2 + 1, :]
                        picks.append(jnp.where(slot_row == slot_rows, gate_row, 0.0).astype(jnp.bfloat16))
                    picked = jnp.dot(
                        jnp.concatenate(picks, axis=0), xbuf[block], preferred_element_type=jnp.float32
                    ).astype(jnp.bfloat16)
                    to = pl.ds(pl.multiple_of((i * pick_blocks + n) * cap, cap), cap)
                    for j in range(experts):
                        sbuf[j, to, :] = picked[j * cap : (j + 1) * cap]

            for m in range(PARTS):
                @pl.when((p > 0) & (i == 4 + m))
                def _():
                    left = slice(m * part_width, (m + 1) * part_width)
                    right = slice(width + m * part_width, width + (m + 1) * part_width)
                    for j in range(experts):
                        row_grad = lax.dot_general(
                            sbuf[j], wbuf[j, left], (((1,), (1,)), ((), ())), preferred_element_type=jnp.float32
                        )
                        silu = fs[j, at, left]
                        hidden = (silu * pbuf[j, at, right].astype(jnp.float32)).astype(jnp.bfloat16)
                        obuf[j, at, left] = (row_grad * fa[j, at, left]).astype(jnp.bfloat16)
                        obuf[j, at, right] = (row_grad * silu).astype(jnp.bfloat16)
                        score = jnp.sum(hidden.astype(jnp.float32) * row_grad, axis=1, keepdims=True)
                        score = jnp.broadcast_to(score, (layer_rows, tok))
                        scores[j] = score if m == 0 else scores[j] + score

            @pl.when((p > 0) & (i == 4 + PARTS))
            def _():
                for n in range(near_blocks):
                    block = ready * near_blocks + n
                    for j in range(experts):
                        slot_row = tab[block, j * REPEAT + REPEAT // 2 : j * REPEAT + REPEAT // 2 + 1, :]
                        values = jnp.sum(
                            jnp.where(slot_row == slot_rows, scores[j, n * cap : (n + 1) * cap, :], 0.0),
                            axis=0,
                            keepdims=True,
                        )
                        ts_out[block, j * REPEAT : (j + 1) * REPEAT, :] = jnp.broadcast_to(values, (REPEAT, tok))
                    pltpu.make_async_remote_copy(
                        src_ref=ts_out.at[block], dst_ref=ts_in.at[me], send_sem=ts_send.at[0], recv_sem=ts_recv.at[0],
                        device_id=(before, block), device_id_type=MESH,
                    ).start()
                pltpu.make_async_copy(obuf.at[:, at, :], out_ref.at[:, at, :], out_sem.at[ready]).start()
            return inner

        lax.fori_loop(0, CHUNKS, step, 0)
        return carry

    lax.fori_loop(0, LAYERS + 1, round_of, 0)

    for copy in near:
        copy.wait_recv()
    gate = jnp.zeros((groups * tile, tok), jnp.float32)
    for k in range(top):
        gate = jnp.where(nids[k : k + 1, :] == row_expert, ngates[k : k + 1, :], gate)
    full_gate[...] = gate
    pltpu.make_async_copy(rbuf, rbuf, router_recv.at[0]).wait()
    pltpu.make_async_copy(ts_in, ts_in, ts_recv.at[0]).wait()
    gate = full_gate[...]
    gate_low = gate.astype(jnp.bfloat16).astype(jnp.float32)
    scaled_score = ts_in[...].reshape(groups * tile, tok)
    score = jnp.where(gate_low > 0.0, scaled_score / jnp.where(gate_low > 0.0, gate_low, 1.0), 0.0)
    total = jnp.sum(jnp.where(rows % REPEAT == 0, gate * score, 0.0), axis=0, keepdims=True)
    logit = jnp.transpose(gate * (score - total))
    lanes = lax.broadcasted_iota(jnp.int32, (tok, groups * tile), 1) % REPEAT
    router = rbuf[...].reshape(groups * tile, part)
    for d in range(REPEAT):
        left = jnp.where(lanes == d, logit, 0.0).astype(jnp.bfloat16)
        change = jnp.dot(left, router, preferred_element_type=jnp.float32)
        at = slice(d * part, (d + 1) * part)
        gbuf[:, at] = (nbuf[:, at].astype(jnp.float32) + change).astype(jnp.bfloat16)
    store = pltpu.make_async_copy(gbuf, grad_ref, local_sem.at[3])
    store.start()

    def all_sent(blocks, count, sem):
        view = xbuf.at[pl.ds(0, blocks), pl.ds(0, count)]
        pltpu.make_async_copy(view, view, x_send.at[sem]).wait()

    all_sent(groups // 2, tok, SIB)
    if wide > 1:
        all_sent(wide - 1, tok, OWN_SIDE)
        all_sent((LAYERS - 1) * (wide - 1), tok - chunk, SIDE)
    for n in range(LAYERS):
        @pl.when(layer == n)
        def _():
            if n < LAYERS - 1:
                all_sent(n + 1, tok, UP)
                if wide > 1:
                    all_sent((n + 1) * (wide - 1), chunk, SIDE_UP)
            if n > 0:
                all_sent(LAYERS - n, tok, UP + 1)
                if wide > 1:
                    all_sent((LAYERS - n) * (wide - 1), chunk, SIDE_UP + 1)
    pltpu.make_async_copy(own_tab.at[pl.ds(0, groups - 1)], tab.at[pl.ds(0, groups - 1)], tab_send.at[0]).wait()
    for copy in near:
        copy.wait_send()
    pltpu.make_async_copy(rbuf, rbuf, router_send.at[0]).wait()
    pltpu.make_async_copy(ts_in, ts_in, ts_send.at[0]).wait()
    for n in range(LAYERS):
        at = pl.ds(n * layer_rows, layer_rows)
        pltpu.make_async_copy(obuf.at[:, at, :], out_ref.at[:, at, :], out_sem.at[n]).wait()
    store.wait()


def per_device(grad_out, expert_ids, slot_ids, gate_weights, saved_pre, down_weight, router_weight):
    groups = lax.axis_size("expert")
    pipes = lax.axis_size("pipe")
    _, experts, width, features = down_weight.shape
    slots = saved_pre.shape[2]
    tok = grad_out.shape[1]
    top = expert_ids.shape[2]
    cap = slots // groups
    layer_rows = slots // LAYERS
    tile = experts * REPEAT
    part = features // REPEAT
    bf16, f32 = jnp.bfloat16, jnp.float32
    dma = pltpu.SemaphoreType.DMA
    vmem = pl.BlockSpec(memory_space=pltpu.VMEM)
    anywhere = pl.BlockSpec(memory_space=pl.ANY)
    pre_grad, grad_inputs = pl.pallas_call(
        functools.partial(kernel, groups, pipes, cap),
        out_shape=(
            jax.ShapeDtypeStruct((experts, slots, 2 * width), bf16),
            jax.ShapeDtypeStruct((tok, features), bf16),
        ),
        in_specs=[vmem, vmem, vmem, anywhere, vmem, anywhere, anywhere],
        out_specs=(anywhere, anywhere),
        scratch_shapes=[
            pltpu.VMEM((groups, tok, features), bf16),
            pltpu.VMEM((experts, width, features), bf16),
            pltpu.VMEM((experts, slots, 2 * width), bf16),
            pltpu.VMEM((experts, slots, width), f32),
            pltpu.VMEM((experts, slots, width), f32),
            pltpu.VMEM((experts, layer_rows, features), bf16),
            pltpu.VMEM((experts, slots, 2 * width), bf16),
            pltpu.VMEM((tok, features), bf16),
            pltpu.VMEM((tok, features), bf16),
            pltpu.VMEM((top, tok), jnp.int32),
            pltpu.VMEM((top, tok), f32),
            pltpu.VMEM((groups, tile, part), bf16),
            pltpu.VMEM((groups, tile, tok), f32),
            pltpu.VMEM((groups, tile, tok), f32),
            pltpu.VMEM((groups, tile, tok), f32),
            pltpu.VMEM((groups, tile, tok), f32),
            pltpu.VMEM((groups * tile, tok), f32),
            pltpu.VMEM((experts, layer_rows, tok), f32),
            pltpu.VMEM((tile, part), bf16),
            dma((4,)),
            dma((LAYERS,)),
            dma((7,)),
            dma((groups, CHUNKS)),
            dma((groups,)),
            dma((1,)),
            dma((1,)),
            dma((3,)),
            dma((3,)),
            dma((1,)),
            dma((1,)),
            dma((1,)),
            dma((1,)),
        ],
        compiler_params=pltpu.CompilerParams(
            collective_id=0, has_side_effects=True, vmem_limit_bytes=56 * 1024 * 1024
        ),
        cost_estimate=pl.CostEstimate(
            flops=2 * experts * slots * width * features, bytes_accessed=16 * 1024 * 1024, transcendentals=0
        ),
    )(
        expert_ids[0].T,
        slot_ids[0].T,
        gate_weights[0].T,
        grad_out[0],
        router_weight[0],
        saved_pre[0],
        down_weight[0],
    )
    return (pre_grad[None], grad_inputs[None])


def solution(mesh):
    in_specs = (
        P("pipe", "expert", None),
        P("pipe", "expert", None),
        P("pipe", "expert", None),
        P("pipe", "expert", None),
        P("pipe", "expert", None, None),
        P("pipe", "expert", None, None),
        P("pipe", "expert", None),
    )
    out_specs = (P("pipe", "expert", None, None), P("pipe", "expert", None))
    return jax.shard_map(
        per_device, mesh=mesh, in_specs=in_specs, out_specs=out_specs, check_vma=False
    )
```
